256 devices in a mesh: ctx: 32 (over y, x, z_hi), head: 8 (over z_lo, core).
Axes of the slice: x: 4, y: 4, z: 8 (z_hi: 2, z_lo: 4; z = z_hi * 4 + z_lo), core: 2. Of those that a mesh axis runs over, the one named last changes fastest.
Arguments:
- queries: bfloat16 [16384, 3072], P(('ctx', 'head')), may hold values from -200 to 200
- keys: bfloat16 [16384, 3072], P(('ctx', 'head')), may hold values from -18 to 18
- values: bfloat16 [16384, 3072], P(('ctx', 'head')), may hold values from -6 to 6
- residual: bfloat16 [16384, 3072], P(('ctx', 'head')), may hold values from -6 to 6
- out_weight: bfloat16 [3072, 3072], P('head'), may hold values from -0.4375 to 0.4375
- gate_table: float32 [8, 3072], replicated, may hold values from 0.3 to 3
- span_lengths: int32 [4], replicated, may hold values from 1 to 8192, 16384 in all
- noise_levels: int32 [4], replicated, may hold values from 0 to 7
Outputs:
- mixed: bfloat16 [16384, 3072], P(('ctx', 'head'))
The draws below stay inside these ranges and needn't reach their ends.
Inputs may be any that keep to these rules, and one draw needn't show every extreme that they name: `span_lengths`: 4 positive lengths that sum to 16384; the largest is 8192.
All inputs are finite; a program needn't handle non-finite values.
Results may differ from the reference program's by a relative error of at most 0.024.
Values may be sent and summed in bfloat16 or wider, within the bound.
No kernel may reach another device: no remote copies, remote signals or barrier semaphores. Data moves between devices by JAX's collectives and lax.ppermute only.
A program may use at most 192 MiB of HBM per device.

```python
import math
import jax
import jax.numpy as jnp
import numpy as np
from jax import lax

D = 3072
HEADS = 24
HEAD_DIM = 128
SPANS = 4
LEVELS = 8
SEQ = 16384
N_HEAD = 8


def shape_keys(key):
    base = jnp.clip(1.5 * jax.random.normal(key, (SEQ, HEADS * HEAD_DIM), jnp.float32), -6.0, 6.0)
    scaled = base
    return scaled


def draw_keys(key, part):
    return shape_keys(key).astype(jnp.bfloat16)


def draw_queries(key, part):
    own_key = jax.random.fold_in(key, 3)
    fresh = jnp.clip(1.5 * jax.random.normal(own_key, (SEQ, HEADS * HEAD_DIM), jnp.float32), -6.0, 6.0)
    return fresh.astype(jnp.bfloat16)


def set_ends(values, stream_key, low, top_value):
    index_at = [jax.random.randint(jax.random.fold_in(stream_key, axis), (), 0, length) for axis, length in enumerate(values.shape)]
    widest = values.shape.index(max(values.shape))
    neighbour = index_at[:widest] + [(index_at[widest] + 1) % values.shape[widest]] + index_at[widest + 1:]
    return values.at[tuple(index_at)].set(low).at[tuple(neighbour)].set(top_value)


def shard_levels(rng, shape, split, low, largest):
    def one(position, blocks):
        draws = jax.random.uniform(jax.random.fold_in(jax.random.fold_in(rng, 6), position), (blocks,), jnp.float32, low / len(split), largest / len(split))
        return jnp.repeat(jnp.exp(draws), shape[position] // blocks).reshape((-1,) + (1,) * (len(shape) - position - 1))

    loudness = one(*split[0])
    for cut in split[1:]:
        loudness = loudness * one(*cut)
    return loudness


def profile(count, total, reach, skew):
    portions = [(1 << 20) // math.isqrt(rank ** skew) + 1 for rank in range(2, count + 1)]
    rest, holding = total - reach - (count - 1), [1] * (count - 1)
    while rest > 0:
        candidates = [i for i in range(count - 1) if holding[i] < reach]
        pool, budget = sum([portions[i] for i in candidates]), rest
        for i in candidates:
            addition = min(reach - holding[i], max(1, budget * portions[i] // pool), rest)
            holding[i] = holding[i] + addition
            rest = rest - addition
    return np.array([reach] + holding)


def ragged_sizes(key, number_of, total, reach, lean):
    if number_of == 2:
        one = jax.random.randint(key, (), max(1, total - reach), min(reach, total - 1) + 1)
        return jnp.stack([one, total - one])
    lengths = jnp.asarray(profile(number_of, total, reach, lean), jnp.int32)
    twos = (number_of - 1) // 2
    giver, sink = lengths[1:1 + 2 * twos:2], lengths[2:2 + 2 * twos:2]
    slack = jnp.minimum(giver - 1, reach - sink)
    passed = jax.random.randint(jax.random.fold_in(key, 1), (twos,), 0, 1 << 20) % (slack + 1)
    lengths = lengths.at[1:1 + 2 * twos:2].set(giver - passed).at[2:2 + 2 * twos:2].set(sink + passed)
    return lengths[jax.random.permutation(jax.random.fold_in(key, 2), number_of)]


def normal_values(key, extent, scale, bound, cuts=(), kind=jnp.bfloat16):
    gain = shard_levels(key, extent, cuts, -0.22, 0.18) if cuts else 1.0
    array = jax.random.normal(key, extent, jnp.float32) * scale * gain
    return jnp.minimum(jnp.maximum(array, -bound), bound).astype(kind)


def setup_inputs(seed: int = 0) -> dict:
    splits = jax.random.split(jax.random.key(seed), 9)
    return {
        "queries": draw_queries(jax.random.fold_in(splits[8], 71), 0),
        "keys": draw_keys(jax.random.fold_in(splits[8], 71), 0),
        "values": normal_values(splits[2], (SEQ, HEADS * HEAD_DIM), 1.0, 6.0, ((0, 256),)),
        "residual": normal_values(splits[3], (SEQ, D), 1.0, 6.0, ((0, 256),)),
        "out_weight": normal_values(splits[4], (HEADS * HEAD_DIM, D), (HEADS * HEAD_DIM // 16) ** -0.5, 0.4375, ((0, 8),)),
        "gate_table": jnp.clip(jnp.exp(jax.random.uniform(splits[5], (LEVELS, D), jnp.float32, math.log(0.3), math.log(3.0))), 0.3, 3.0),
        "span_lengths": ragged_sizes(splits[6], SPANS, SEQ, SEQ // 2, 2).astype(jnp.int32),
        "noise_levels": set_ends(jax.random.randint(splits[7], (SPANS,), 0, LEVELS), jax.random.fold_in(splits[7], 1), 0, LEVELS - 1).astype(jnp.int32),
    }


def reference(queries, keys, values, residual, out_weight, gate_table, span_lengths, noise_levels):
    seq = queries.shape[0]
    ends = jnp.cumsum(span_lengths)
    positions = jnp.arange(seq, dtype=jnp.int32)
    span_of = jnp.sum((positions[:, None] >= ends[None, :]).astype(jnp.int32), axis=1)
    block = 512 if seq % 512 == 0 else seq
    count = seq // block
    scale = HEAD_DIM ** -0.5
    q_heads = queries.reshape(seq, HEADS, HEAD_DIM).transpose(1, 0, 2)
    k_heads = keys.reshape(seq, HEADS, HEAD_DIM).transpose(1, 0, 2)
    v_heads = values.reshape(seq, HEADS, HEAD_DIM).transpose(1, 0, 2)
    q_spans = span_of.reshape(count, block)

    def one_head(operands):
        q_one, k_one, v_one = operands
        q_blocks = q_one.reshape(count, block, HEAD_DIM)

        def one_block(inner):
            q_blk, c_blk = inner
            scores = jnp.dot(q_blk, k_one.T, preferred_element_type=jnp.float32) * scale
            visible = span_of[None, :] <= c_blk[:, None]
            peak = jnp.max(jnp.where(visible, scores, -jnp.inf), axis=1)
            weight = jnp.where(visible, jnp.exp(scores - peak[:, None]), 0.0)
            total = jnp.sum(weight, axis=1)
            summed = jnp.dot(weight.astype(jnp.bfloat16), v_one, preferred_element_type=jnp.float32)
            return (summed / total[:, None]).astype(jnp.bfloat16)

        return lax.map(one_block, (q_blocks, q_spans)).reshape(seq, HEAD_DIM)

    attn = lax.map(one_head, (q_heads, k_heads, v_heads))
    attn = attn.transpose(1, 0, 2).reshape(seq, HEADS * HEAD_DIM)
    width = (HEADS // N_HEAD) * HEAD_DIM
    proj = jnp.zeros((seq, out_weight.shape[1]), jnp.float32)
    for group in range(N_HEAD):
        term = jnp.dot(attn[:, group * width:(group + 1) * width], out_weight[group * width:(group + 1) * width], preferred_element_type=jnp.float32)
        rounded = lax.optimization_barrier(term.astype(jnp.bfloat16))
        proj = proj + rounded.astype(jnp.float32)
    gate = gate_table[noise_levels[span_of]]
    return (residual.astype(jnp.float32) + gate * proj).astype(jnp.bfloat16)
```

```python
import jax
import jax.numpy as jnp
from jax import lax
from jax.sharding import Mesh, PartitionSpec as P
from jax.experimental import pallas as pl
from jax.experimental.pallas import tpu as pltpu

HD = 128
PER = 3
W = PER * HD
TOK = 64
SCALE2 = HD ** (-0.5) * 1.4426950408889634
NEG = -1e30
NY, NX, NZ, NC = 4, 4, 8, 2
QT = 256
KT = 512
ROWS = TOK + 8


def attention_kernel(ends_ref, pos_ref, *refs):
    q_in = refs[0:4]
    kv_in = refs[4:14]
    o_ref, lse_ref = refs[14:16]
    q_s, kv_s, qt_s, m_s, l_s, acc_s, sems = refs[16:]
    y, x, zl, core = pos_ref[0], pos_ref[1], pos_ref[2], pos_ref[3]
    y0 = lax.rem(y - zl + NY, NY)
    copies = []
    for j, step in enumerate((0, 1, 3, 2)):
        copies.append((q_in[j], q_s.at[lax.rem(x + step, NX)]))
    half = KT // 2
    for s in range(2):
        side = core if s == 0 else 1 - core
        at = pl.ds(pl.multiple_of(side * half, half), half)
        base = 5 * s
        for j, step in enumerate((0, 1, 3)):
            slot = lax.rem(y + step, NY) * 2
            for hi in range(2):
                copies.append((kv_in[base + j].at[pl.ds(hi * half, half)], kv_s.at[slot + hi, at]))
        slot = lax.rem(y + 2, NY) * 2
        for hi in range(2):
            copies.append((kv_in[base + 3 + hi], kv_s.at[slot + hi, at]))
    started = []
    for n, (src, dst) in enumerate(copies):
        c = pltpu.make_async_copy(src, dst, sems.at[n])
        c.start()
        started.append(c)
    for c in started:
        c.wait()

    def limit_of(p):
        out = ends_ref[3]
        for j in (2, 1, 0):
            out = jnp.where(p < ends_ref[j], ends_ref[j], out)
        return out

    def tile(t, carry):
        quarter_z = lax.div(t, 2)
        pair = lax.rem(t, 2)
        quarter = lax.rem(y0 + quarter_z, NY)
        first = quarter * 4096 + pair * 2048 + quarter_z * 128 + core * TOK
        low, high = limit_of(first), limit_of(first + 1599)
        full, seen = jnp.int32(0), jnp.int32(0)
        for c in range(8):
            start = (c // 2) * 4096 + (c % 2) * 512 + x * 1024
            full += jnp.where(start + 512 <= low, 1, 0)
            seen += jnp.where(start < high, 1, 0)
        for a in range(2):
            for b in range(2):
                qt_s[pl.ds((a * 2 + b) * TOK, TOK), :] = q_s[
                    2 * pair + a, pl.ds(pl.multiple_of((b * 4 + quarter_z) * TOK, TOK), TOK), :
                ]
        m_s[...] = jnp.full_like(m_s, NEG)
        l_s[...] = jnp.zeros_like(l_s)
        acc_s[...] = jnp.zeros_like(acc_s)

        def chunk(c, masked):
            if masked:
                row = lax.broadcasted_iota(jnp.int32, (QT, HD), 0)
                qpos = first + (row // 128) * 1024 + ((row // TOK) % 2) * 512 + row % TOK
                lim = limit_of(qpos)[:, :1]
                col = lax.broadcasted_iota(jnp.int32, (1, KT), 1)
                start = lax.div(c, 2) * 4096 + lax.rem(c, 2) * 512 + x * 1024
                kpos = start + ((col % 256) // TOK) * 128 + (col // 256) * TOK + col % TOK
                visible = kpos < lim
            for h in range(PER):
                q = qt_s[:, h * HD : (h + 1) * HD]
                k = kv_s[c, :, h * HD : (h + 1) * HD]
                v = kv_s[c, :, W + h * HD : W + (h + 1) * HD]
                s = lax.dot_general(q, k, (((1,), (1,)), ((), ())), preferred_element_type=jnp.float32)
                if masked:
                    s = jnp.where(visible, s, NEG)
                old = m_s[h]
                new = jnp.maximum(old, jnp.max(s, axis=1, keepdims=True))
                fade = jnp.exp2((old - new) * SCALE2)
                p = jnp.exp2((s - jnp.concatenate([new] * (KT // HD), axis=1)) * SCALE2)
                part = p[:, :HD]
                for g in range(1, KT // HD):
                    part = part + p[:, g * HD : (g + 1) * HD]
                l_s[h] = l_s[h] * fade + part
                acc_s[h] = acc_s[h] * fade + jnp.dot(
                    p.astype(jnp.bfloat16), v, preferred_element_type=jnp.float32
                )
                m_s[h] = new

        def full_chunk(c, carry):
            chunk(c, False)
            return carry

        def masked_chunk(c, carry):
            chunk(c, True)
            return carry

        lax.fori_loop(0, full, full_chunk, 0)
        lax.fori_loop(full, seen, masked_chunk, 0)
        lane = lax.broadcasted_iota(jnp.int32, (QT, HD), 1)
        lse = jnp.zeros((QT, HD), jnp.float32)
        for h in range(PER):
            total = jnp.sum(l_s[h], axis=1, keepdims=True)
            total = jnp.where(total == 0.0, 1.0, total)
            out = (acc_s[h] / total).astype(jnp.bfloat16)
            for a in range(2):
                for b in range(2):
                    o_ref[2 * pair + a, b * 4 + quarter_z, :, h * HD : (h + 1) * HD] = out[
                        (a * 2 + b) * TOK : (a * 2 + b + 1) * TOK
                    ]
            lse = jnp.where(lane == h, m_s[h] * SCALE2 + jnp.log2(total), lse)
        for a in range(2):
            for b in range(2):
                lse_ref[2 * pair + a, b * 4 + quarter_z] = lse[(a * 2 + b) * TOK : (a * 2 + b + 1) * TOK]
        return carry

    lax.fori_loop(0, 8, tile, 0)


def attention(ends, place, qs, kvs):
    n_copies = 4 + 16
    hbm = pl.BlockSpec(memory_space=pl.ANY)
    smem = pl.BlockSpec(memory_space=pltpu.SMEM)
    vmem = pl.BlockSpec(memory_space=pltpu.VMEM)
    return pl.pallas_call(
        attention_kernel,
        out_shape=(
            jax.ShapeDtypeStruct((NX, NZ, TOK, W), jnp.bfloat16),
            jax.ShapeDtypeStruct((NX, NZ, TOK, HD), jnp.float32),
        ),
        in_specs=[smem, smem] + [hbm] * 14,
        out_specs=(vmem, vmem),
        scratch_shapes=[
            pltpu.VMEM((NX, NZ * TOK, W), jnp.bfloat16),
            pltpu.VMEM((8, KT, 2 * W), jnp.bfloat16),
            pltpu.VMEM((QT, W), jnp.bfloat16),
            pltpu.VMEM((PER, QT, HD), jnp.float32),
            pltpu.VMEM((PER, QT, HD), jnp.float32),
            pltpu.VMEM((PER, QT, HD), jnp.float32),
            pltpu.SemaphoreType.DMA((n_copies,)),
        ],
        compiler_params=pltpu.CompilerParams(vmem_limit_bytes=48 * 1024 * 1024),
        cost_estimate=pl.CostEstimate(
            flops=12_900_000_000, bytes_accessed=10_000_000, transcendentals=25_000_000
        ),
        name="attention",
    )(ends, place, *qs, *kvs)


def ring(a, axis, step):
    return lax.ppermute(a, axis, [((i + step) % 4, i) for i in range(4)])


def swap(a):
    return lax.ppermute(a, "core", [(0, 1), (1, 0)])


SKEW_Q = [[((y0 + z) % NY) * NZ + z for z in range(NZ)] for y0 in range(NY)]
SKEW_O = [
    [(((y0 + z) % NY) * NX + x) * NZ + z for x in range(NX) for z in range(NZ)] for y0 in range(NY)
]


def local(queries, keys, values, residual, out_weight, gate_table, span_lengths, noise_levels):
    def by_group(a):
        return a.reshape(TOK, NZ, W).transpose(1, 0, 2)

    weight = lax.all_gather(out_weight, ("zl", "core"), axis=0, tiled=True)
    kv = jnp.concatenate([by_group(keys), by_group(values)], axis=2)
    kv = lax.all_to_all(kv, ("zh", "zl"), 0, 0, tiled=True).reshape(NZ * TOK, 2 * W)
    q = lax.all_to_all(
        by_group(queries), ("y", "zh", "zl"), 0, 0, tiled=True, axis_index_groups=SKEW_Q
    ).reshape(NZ * TOK, W)
    kv_p, kv_m = ring(kv, "y", 1), ring(kv, "y", 3)
    half = NZ * TOK // 2
    kv_2a = ring(kv_p[:half], "y", 1)
    kv_2b = ring(kv_m[half:], "y", 3)
    mine = [kv, kv_p, kv_m, kv_2a, kv_2b]
    other = [swap(a) for a in mine]
    q_p, q_m = ring(q, "x", 1), ring(q, "x", 3)
    q_2 = ring(q_p, "x", 1)
    ends = jnp.cumsum(span_lengths)
    y, x, zl, core = (lax.axis_index(n) for n in ("y", "x", "zl", "core"))
    z = lax.axis_index(("zh", "zl"))
    place = jnp.stack([y, x, zl, core]).astype(jnp.int32)
    out, lse = attention(ends, place, [q, q_p, q_m, q_2], mine + other)
    stat = lse[..., :PER]
    s1 = lax.reduce_precision(stat, 8, 7)
    r1 = stat - s1
    s2 = lax.reduce_precision(r1, 8, 7)
    s3 = r1 - s2
    stats = jnp.stack([s1, s2, s3], axis=2).astype(jnp.bfloat16)
    stats = stats.transpose(0, 1, 2, 4, 3).reshape(NX, NZ, 3 * PER * TOK)
    stats = jnp.pad(stats, ((0, 0), (0, 0), (0, 8 * W - 3 * PER * TOK))).reshape(NX, NZ, 8, W)
    sent = jnp.concatenate([out, stats], axis=2).reshape(NX * NZ, ROWS, W)
    got = lax.all_to_all(
        sent, ("y", "x", "zh", "zl"), 0, 0, tiled=True, axis_index_groups=SKEW_O
    ).reshape(NX, NZ, ROWS, W)
    part = got[:, :, :TOK].reshape(NX, NZ, TOK, PER, HD).astype(jnp.float32)
    stat = got[:, :, TOK:].reshape(NX, NZ, 8 * W)[:, :, : 3 * PER * TOK]
    stat = jnp.sum(stat.reshape(NX, NZ, 3, PER, TOK).astype(jnp.float32), axis=2)
    share = jnp.exp2(stat - jnp.max(stat, axis=0, keepdims=True))
    share = share / jnp.sum(share, axis=0, keepdims=True)
    share = share.transpose(0, 1, 3, 2)[..., None]
    attn = jnp.sum(part * share, axis=0).astype(jnp.bfloat16)
    attn = attn.transpose(1, 0, 2, 3).reshape(TOK, NZ * W)
    proj = jnp.dot(attn, weight, preferred_element_type=jnp.float32)
    first = (((y * NX + x) * NZ + z) * NC + core) * TOK
    tok = first + jnp.arange(TOK, dtype=jnp.int32)
    tok_span = jnp.sum((tok[:, None] >= ends[None, :]).astype(jnp.int32), axis=1)
    span_ids = jnp.arange(span_lengths.shape[0], dtype=jnp.int32)
    level = jnp.sum(jnp.where(tok_span[:, None] == span_ids[None, :], noise_levels[None, :], 0), axis=1)
    level_ids = jnp.arange(gate_table.shape[0], dtype=jnp.int32)
    one_hot = (level[:, None] == level_ids[None, :]).astype(jnp.float32)
    gate = jnp.dot(one_hot, gate_table, precision=lax.Precision.HIGHEST)
    return (residual.astype(jnp.float32) + gate * proj).astype(jnp.bfloat16)


def solution(mesh):
    fine = Mesh(mesh.devices.reshape(NY, NX, 2, 4, NC), ("y", "x", "zh", "zl", "core"))
    rows = P(("y", "x", "zh", "zl", "core"), None)
    return jax.shard_map(
        local,
        mesh=fine,
        in_specs=(rows, rows, rows, rows, P(("zl", "core"), None), P(), P(), P()),
        out_specs=rows,
        check_vma=False,
    )
```

```python
import jax
import jax.numpy as jnp
from jax import lax
from jax.sharding import Mesh, PartitionSpec as P
from jax.experimental import pallas as pl
from jax.experimental.pallas import tpu as pltpu

HD = 128
PER = 3
W = PER * HD
TOK = 64
SCALE2 = HD ** (-0.5) * 1.4426950408889634
NEG = -1e30
NY, NX, NZ, NC = 4, 4, 8, 2
NXT = 2
QT = NXT * 2 * TOK
KT = 512
PAIR = 2
QROWS = NZ * TOK
SROWS = 32
ROWS = QROWS + SROWS
D = 3072


def attention_kernel(ends_ref, pos_ref, *refs):
    q_in = refs[0]
    kv_in = refs[1:11]
    o_ref = refs[11]
    q_s, kv_s, qt_s, m_s, l_s, acc_s, lse_s, sems = refs[12:]
    y, x, zl, core = pos_ref[0], pos_ref[1], pos_ref[2], pos_ref[3]
    y0 = lax.rem(y - zl + NY, NY)
    copies = [(q_in, q_s)]
    for s in range(2):
        side = core if s == 0 else 1 - core
        base = 5 * s
        for j, step in enumerate((0, 1, 3, 2)):
            for n in range(NZ):
                quarter = lax.rem(y0 + step + n, NY)
                at = (quarter * 2 + n // 4) * KT + side * (KT // 2) + (n % 4) * TOK
                dst = kv_s.at[pl.ds(pl.multiple_of(at, TOK), TOK)]
                if j < 3:
                    src = kv_in[base + j].at[pl.ds(n * TOK, TOK)]
                else:
                    src = kv_in[base + 3 + n // 4].at[pl.ds((n % 4) * TOK, TOK)]
                copies.append((src, dst))
    started = []
    for n, (src, dst) in enumerate(copies):
        c = pltpu.make_async_copy(src, dst, sems.at[n])
        c.start()
        started.append(c)
    for c in started:
        c.wait()

    def limit_of(p):
        out = ends_ref[3]
        for j in (2, 1, 0):
            out = jnp.where(p < ends_ref[j], ends_ref[j], out)
        return out

    def tile(t, carry):
        quarter_z = lax.div(t, NX // NXT)
        part_x = lax.rem(t, NX // NXT) * NXT
        quarter = lax.rem(y0 + quarter_z, NY)
        first = quarter * 4096 + part_x * 1024 + quarter_z * 128 + core * TOK
        low, high = limit_of(first), limit_of(first + (NXT - 1) * 1024 + 512 + TOK - 1)
        full, seen = jnp.int32(0), jnp.int32(0)
        for c in range(8):
            start = (c // 2) * 4096 + (c % 2) * 512 + x * 1024
            full += jnp.where(start + 512 <= low, 1, 0)
            seen += jnp.where(start < high, 1, 0)
        for a in range(NXT):
            for b in range(2):
                qt_s[pl.ds((a * 2 + b) * TOK, TOK), :] = q_s[
                    part_x + a, pl.ds(pl.multiple_of((b * 4 + quarter_z) * TOK, TOK), TOK), :
                ]
        m_s[...] = jnp.full_like(m_s, NEG)
        l_s[...] = jnp.zeros_like(l_s)
        acc_s[...] = jnp.zeros_like(acc_s)

        def chunk(c, size, masked):
            keys = size * KT
            rows = pl.ds(pl.multiple_of(c * KT, KT), keys)
            if masked:
                row = lax.broadcasted_iota(jnp.int32, (QT, HD), 0)
                qpos = first + (row // 128) * 1024 + ((row // TOK) % 2) * 512 + row % TOK
                lim = limit_of(qpos)[:, :1]
                col = lax.broadcasted_iota(jnp.int32, (1, KT), 1)
                start = lax.div(c, 2) * 4096 + lax.rem(c, 2) * 512 + x * 1024
                kpos = start + ((col % 256) // TOK) * 128 + (col // 256) * TOK + col % TOK
                visible = kpos < lim

            def score(h):
                q = qt_s[:, h * HD : (h + 1) * HD]
                k = kv_s[rows, h * HD : (h + 1) * HD]
                return lax.dot_general(q, k, (((1,), (1,)), ((), ())), preferred_element_type=jnp.float32)

            ahead = score(0)
            for h in range(PER):
                s = ahead
                if h + 1 < PER:
                    ahead = score(h + 1)
                v = kv_s[rows, W + h * HD : W + (h + 1) * HD]
                if masked:
                    s = jnp.where(visible, s, NEG)
                old = m_s[h]
                new = jnp.maximum(old, jnp.max(s, axis=1, keepdims=True))
                fade = jnp.exp2((old - new) * SCALE2)
                p = jnp.exp2((s - jnp.concatenate([new] * (keys // HD), axis=1)) * SCALE2)
                part = p[:, :HD]
                for g in range(1, keys // HD):
                    part = part + p[:, g * HD : (g + 1) * HD]
                l_s[h] = l_s[h] * fade + part
                acc_s[h] = acc_s[h] * fade + jnp.dot(
                    p.astype(jnp.bfloat16), v, preferred_element_type=jnp.float32
                )
                m_s[h] = new

        def full_chunk(c, carry):
            chunk(c * PAIR, PAIR, False)
            return carry

        def masked_chunk(c, carry):
            chunk(c, 1, True)
            return carry

        whole = lax.div(full, PAIR)
        lax.fori_loop(0, whole, full_chunk, 0)
        lax.fori_loop(whole * PAIR, seen, masked_chunk, 0)
        lane = lax.broadcasted_iota(jnp.int32, (QT, HD), 1)
        lse = jnp.zeros((QT, HD), jnp.float32)
        for h in range(PER):
            total = jnp.sum(l_s[h], axis=1, keepdims=True)
            total = jnp.where(total == 0.0, 1.0, total)
            out = (acc_s[h] / total).astype(jnp.bfloat16)
            for a in range(NXT):
                for b in range(2):
                    at = pl.ds(pl.multiple_of((b * 4 + quarter_z) * TOK, TOK), TOK)
                    o_ref[part_x + a, at, h * HD : (h + 1) * HD] = out[
                        (a * 2 + b) * TOK : (a * 2 + b + 1) * TOK
                    ]
            lse = jnp.where(lane == h, m_s[h] * SCALE2 + jnp.log2(total), lse)
        for a in range(NXT):
            for b in range(2):
                at = pl.ds(pl.multiple_of((b * 4 + quarter_z) * TOK, TOK), TOK)
                lse_s[part_x + a, at, :] = lse[(a * 2 + b) * TOK : (a * 2 + b + 1) * TOK]
        return carry

    lax.fori_loop(0, 4 * NX // NXT, tile, 0)
    for a in range(NX):
        stat = jnp.concatenate(
            [lse_s[a, g * HD : (g + 1) * HD, :].T[:8] for g in range(QROWS // HD)], axis=0
        )
        for n in range(3):
            part = stat.astype(jnp.bfloat16)
            o_ref[a, QROWS:, n * HD : (n + 1) * HD] = part
            stat = stat - part.astype(jnp.float32)


def attention(ends, place, q_all, kvs):
    n_copies = 1 + 64
    hbm = pl.BlockSpec(memory_space=pl.ANY)
    smem = pl.BlockSpec(memory_space=pltpu.SMEM)
    vmem = pl.BlockSpec(memory_space=pltpu.VMEM)
    return pl.pallas_call(
        attention_kernel,
        out_shape=jax.ShapeDtypeStruct((NX, ROWS, W), jnp.bfloat16),
        in_specs=[smem, smem] + [hbm] * 11,
        out_specs=vmem,
        scratch_shapes=[
            pltpu.VMEM((NX, QROWS, W), jnp.bfloat16),
            pltpu.VMEM((8 * KT, 2 * W), jnp.bfloat16),
            pltpu.VMEM((QT, W), jnp.bfloat16),
            pltpu.VMEM((PER, QT, HD), jnp.float32),
            pltpu.VMEM((PER, QT, HD), jnp.float32),
            pltpu.VMEM((PER, QT, HD), jnp.float32),
            pltpu.VMEM((NX, QROWS, HD), jnp.float32),
            pltpu.SemaphoreType.DMA((n_copies,)),
        ],
        compiler_params=pltpu.CompilerParams(vmem_limit_bytes=48 * 1024 * 1024),
        cost_estimate=pl.CostEstimate(
            flops=1_000_000, bytes_accessed=1_000_000, transcendentals=1_000
        ),
        name="attention",
    )(ends, place, q_all, *kvs)


def combine_kernel(got_ref, o_ref):
    logs = []
    for j in range(NX):
        parts = got_ref[j, QROWS:, :].astype(jnp.float32)
        logs.append(parts[:, :HD] + parts[:, HD : 2 * HD] + parts[:, 2 * HD :])
    peak = jnp.maximum(jnp.maximum(logs[0], logs[1]), jnp.maximum(logs[2], logs[3]))
    shares = [jnp.exp2(v - peak) for v in logs]
    total = shares[0] + shares[1] + shares[2] + shares[3]
    shares = [v / total for v in shares]
    for g in range(QROWS // HD):
        rows = [v[g * 8 : (g + 1) * 8] for v in shares]
        columns = jnp.concatenate(rows + [jnp.zeros((HD - 8 * NX, HD), jnp.float32)], axis=0).T
        at = slice(g * HD, (g + 1) * HD)
        for h in range(PER):
            out = jnp.zeros((HD, HD), jnp.float32)
            for j in range(NX):
                part = got_ref[j, at, h * HD : (h + 1) * HD].astype(jnp.float32)
                out = out + part * columns[:, j * 8 + h : j * 8 + h + 1]
            o_ref[at, h * HD : (h + 1) * HD] = out.astype(jnp.bfloat16)


def combine(got):
    vmem = pl.BlockSpec(memory_space=pltpu.VMEM)
    return pl.pallas_call(
        combine_kernel,
        out_shape=jax.ShapeDtypeStruct((QROWS, W), jnp.bfloat16),
        in_specs=[vmem],
        out_specs=vmem,
        compiler_params=pltpu.CompilerParams(vmem_limit_bytes=16 * 1024 * 1024),
        cost_estimate=pl.CostEstimate(flops=4_000_000, bytes_accessed=2_500_000, transcendentals=20_000),
        name="combine",
    )(got)


def project_kernel(pos_ref, keep_ref, got_ref, *refs):
    w_in = refs[:5]
    o_ref = refs[5]
    w_s, acc_s, sems = refs[6:]
    zl = pos_ref[2]
    started = []
    wide = D // 2
    for j in range(5):
        dst = w_s.at[j] if j < 3 else w_s.at[3, :, pl.ds((j - 3) * wide, wide)]
        c = pltpu.make_async_copy(w_in[j], dst, sems.at[j])
        c.start()
        started.append(c)
    acc_s[...] = jnp.zeros_like(acc_s)
    for j, step in enumerate((0, 1, 3, 2)):
        started[j].wait()
        if j == 3:
            started[4].wait()
        row = lax.rem(zl + step, 4)
        lhs = jnp.concatenate([keep_ref[row], got_ref[row]], axis=0)
        acc_s[...] += jnp.dot(lhs, w_s[j], preferred_element_type=jnp.float32)
    o_ref[0] = acc_s[:TOK].astype(jnp.bfloat16)
    o_ref[1] = acc_s[TOK:].astype(jnp.bfloat16)


def project(place, keep, got, weights):
    vmem = pl.BlockSpec(memory_space=pltpu.VMEM)
    return pl.pallas_call(
        project_kernel,
        out_shape=jax.ShapeDtypeStruct((2, TOK, D), jnp.bfloat16),
        in_specs=[pl.BlockSpec(memory_space=pltpu.SMEM), vmem, vmem]
        + [pl.BlockSpec(memory_space=pl.ANY)] * 5,
        out_specs=vmem,
        scratch_shapes=[
            pltpu.VMEM((4, W, D), jnp.bfloat16),
            pltpu.VMEM((2 * TOK, D), jnp.float32),
            pltpu.SemaphoreType.DMA((5,)),
        ],
        compiler_params=pltpu.CompilerParams(vmem_limit_bytes=28 * 1024 * 1024),
        cost_estimate=pl.CostEstimate(
            flops=2 * TOK * D * D, bytes_accessed=10_000_000, transcendentals=0
        ),
        name="project",
    )(place, keep, got, *weights)


def after(token, arrays):
    hbm = pl.BlockSpec(memory_space=pl.ANY)

    def kernel(*refs):
        pass

    return pl.pallas_call(
        kernel,
        out_shape=[jax.ShapeDtypeStruct(a.shape, a.dtype) for a in arrays],
        in_specs=[hbm] * (1 + len(arrays)),
        out_specs=[hbm] * len(arrays),
        input_output_aliases={n + 1: n for n in range(len(arrays))},
        name="after",
    )(token, *arrays)


def ring(a, axis, step):
    return lax.ppermute(a, axis, [((i + step) % 4, i) for i in range(4)])


def swap(a):
    return lax.ppermute(a, "core", [(0, 1), (1, 0)])


SKEW = [[((y0 + z) % NY) * NZ + z for z in range(NZ)] for y0 in range(NY)]


def skewed(a):
    return lax.all_to_all(a, ("y", "zh", "zl"), 0, 0, tiled=True, axis_index_groups=SKEW)


def ring_z(a, step):
    return lax.ppermute(a, ("zh", "zl"), [((i + step) % NZ, i) for i in range(NZ)])


def local(queries, keys, values, residual, out_weight, gate_table, span_lengths, noise_levels):
    def by_group(a):
        return a.reshape(TOK, NZ, W).transpose(1, 0, 2)

    qkv = jnp.concatenate([by_group(queries), by_group(keys), by_group(values)], axis=2)
    qkv = skewed(qkv).reshape(QROWS, 3 * W)
    q, kv = qkv[:, :W], qkv[:, W:]
    kv_p, kv_m = ring(kv, "y", 1), ring(kv, "y", 3)
    half = QROWS // 2
    kv_2a = ring(kv_p[:half], "y", 1)
    kv_2b = ring(kv_m[half:], "y", 3)
    mine = [kv, kv_p, kv_m, kv_2a, kv_2b]
    other = [swap(a) for a in mine]
    q_all = lax.all_to_all(jnp.broadcast_to(q[None], (NX, QROWS, W)), "x", 0, 0, tiled=True)
    arrived = q[0, 0] == q[0, 0]
    w_late = jnp.where(arrived, out_weight, jnp.zeros_like(out_weight))
    w_p, w_m = ring_z(w_late, 1), ring_z(w_late, 7)
    ends = jnp.cumsum(span_lengths)
    y, x, zl, core = (lax.axis_index(n) for n in ("y", "x", "zl", "core"))
    z = lax.axis_index(("zh", "zl"))
    place = jnp.stack([y, x, zl, core]).astype(jnp.int32)
    sent = attention(ends, place, q_all, mine + other)
    w_p, w_m = after(sent, [w_p, w_m])
    w_2a, w_2b = ring_z(w_p[:, : D // 2], 1), ring_z(w_m[:, D // 2 :], 7)
    attn = combine(lax.all_to_all(sent, "x", 0, 0, tiled=True))
    w_2a, w_2b = after(attn, [w_2a, w_2b])
    attn = skewed(attn.reshape(NZ, TOK, W)).reshape(NZ // NC, NC, TOK, W)
    low = core == 0
    keep = jnp.where(low, attn[:, 0], attn[:, 1])
    other_attn = swap(jnp.where(low, attn[:, 1], attn[:, 0]))
    terms = project(place, keep, other_attn, [w_late, w_p, w_m, w_2a, w_2b])
    proj = terms[0].astype(jnp.float32) + swap(terms[1]).astype(jnp.float32)
    first = (((y * NX + x) * NZ + z) * NC + core) * TOK
    tok = first + jnp.arange(TOK, dtype=jnp.int32)
    tok_span = jnp.sum((tok[:, None] >= ends[None, :]).astype(jnp.int32), axis=1)
    span_ids = jnp.arange(span_lengths.shape[0], dtype=jnp.int32)
    level = jnp.sum(jnp.where(tok_span[:, None] == span_ids[None, :], noise_levels[None, :], 0), axis=1)
    level_ids = jnp.arange(gate_table.shape[0], dtype=jnp.int32)
    one_hot = (level[:, None] == level_ids[None, :]).astype(jnp.float32)
    gate = jnp.dot(one_hot, gate_table, precision=lax.Precision.HIGHEST)
    return (residual.astype(jnp.float32) + gate * proj).astype(jnp.bfloat16)


def solution(mesh):
    fine = Mesh(mesh.devices.reshape(NY, NX, 2, 4, NC), ("y", "x", "zh", "zl", "core"))
    rows = P(("y", "x", "zh", "zl", "core"), None)
    return jax.shard_map(
        local,
        mesh=fine,
        in_specs=(rows, rows, rows, rows, P(("zl", "core"), None), P(), P(), P()),
        out_specs=rows,
        check_vma=False,
    )
```

```python
import jax
import jax.numpy as jnp
from jax import lax
from jax.sharding import Mesh, PartitionSpec as P
from jax.experimental import pallas as pl
from jax.experimental.pallas import tpu as pltpu

HD = 128
PER = 3
W = PER * HD
TOK = 64
SCALE2 = HD ** (-0.5) * 1.4426950408889634
NEG = -1e30
NY, NX, NZ, NC = 4, 4, 8, 2
NXT = 2
QT = NXT * 2 * TOK
KT = 512
PAIR = 2
QROWS = NZ * TOK
SROWS = 32
ROWS = QROWS + SROWS
D = 3072


def attention_kernel(ends_ref, pos_ref, *refs):
    q_in = refs[0]
    kv_in = refs[1:11]
    o_ref = refs[11]
    q_s, kv_s, qt_s, m_s, l_s, acc_s, lse_s, sems = refs[12:]
    y, x, zl, core = pos_ref[0], pos_ref[1], pos_ref[2], pos_ref[3]
    y0 = lax.rem(y - zl + NY, NY)
    copies = [(q_in, q_s)]
    for s in range(2):
        side = core if s == 0 else 1 - core
        base = 5 * s
        for j, step in enumerate((0, 1, 3, 2)):
            for n in range(NZ):
                quarter = lax.rem(y0 + step + n, NY)
                at = (quarter * 2 + n // 4) * KT + side * (KT // 2) + (n % 4) * TOK
                dst = kv_s.at[pl.ds(pl.multiple_of(at, TOK), TOK)]
                if j < 3:
                    src = kv_in[base + j].at[pl.ds(n * TOK, TOK)]
                else:
                    src = kv_in[base + 3 + n // 4].at[pl.ds((n % 4) * TOK, TOK)]
                copies.append((src, dst))
    started = []
    for n, (src, dst) in enumerate(copies):
        c = pltpu.make_async_copy(src, dst, sems.at[n])
        c.start()
        started.append(c)
    for c in started:
        c.wait()

    def limit_of(p):
        out = ends_ref[3]
        for j in (2, 1, 0):
            out = jnp.where(p < ends_ref[j], ends_ref[j], out)
        return out

    def tile(t, carry):
        quarter_z = lax.div(t, NX // NXT)
        part_x = lax.rem(t, NX // NXT) * NXT
        quarter = lax.rem(y0 + quarter_z, NY)
        first = quarter * 4096 + part_x * 1024 + quarter_z * 128 + core * TOK
        low, high = limit_of(first), limit_of(first + (NXT - 1) * 1024 + 512 + TOK - 1)
        full, seen = jnp.int32(0), jnp.int32(0)
        for c in range(8):
            start = (c // 2) * 4096 + (c % 2) * 512 + x * 1024
            full += jnp.where(start + 512 <= low, 1, 0)
            seen += jnp.where(start < high, 1, 0)
        for a in range(NXT):
            for b in range(2):
                qt_s[pl.ds((a * 2 + b) * TOK, TOK), :] = q_s[
                    part_x + a, pl.ds(pl.multiple_of((b * 4 + quarter_z) * TOK, TOK), TOK), :
                ]
        m_s[...] = jnp.full_like(m_s, NEG)
        l_s[...] = jnp.zeros_like(l_s)
        acc_s[...] = jnp.zeros_like(acc_s)

        def chunk(c, size, masked):
            keys = size * KT
            rows = pl.ds(pl.multiple_of(c * KT, KT), keys)
            if masked:
                row = lax.broadcasted_iota(jnp.int32, (QT, HD), 0)
                qpos = first + (row // 128) * 1024 + ((row // TOK) % 2) * 512 + row % TOK
                lim = limit_of(qpos)[:, :1]
                col = lax.broadcasted_iota(jnp.int32, (1, KT), 1)
                start = lax.div(c, 2) * 4096 + lax.rem(c, 2) * 512 + x * 1024
                kpos = start + ((col % 256) // TOK) * 128 + (col // 256) * TOK + col % TOK
                visible = kpos < lim

            def score(h):
                q = qt_s[:, h * HD : (h + 1) * HD]
                k = kv_s[rows, h * HD : (h + 1) * HD]
                return lax.dot_general(q, k, (((1,), (1,)), ((), ())), preferred_element_type=jnp.float32)

            ahead = score(0)
            for h in range(PER):
                s = ahead
                if h + 1 < PER:
                    ahead = score(h + 1)
                v = kv_s[rows, W + h * HD : W + (h + 1) * HD]
                if masked:
                    s = jnp.where(visible, s, NEG)
                old = m_s[h]
                new = jnp.maximum(old, jnp.max(s, axis=1, keepdims=True))
                fade = jnp.exp2((old - new) * SCALE2)
                p = jnp.exp2((s - jnp.concatenate([new] * (keys // HD), axis=1)) * SCALE2)
                part = p[:, :HD]
                for g in range(1, keys // HD):
                    part = part + p[:, g * HD : (g + 1) * HD]
                l_s[h] = l_s[h] * fade + part
                acc_s[h] = acc_s[h] * fade + jnp.dot(
                    p.astype(jnp.bfloat16), v, preferred_element_type=jnp.float32
                )
                m_s[h] = new

        def full_chunk(c, carry):
            chunk(c * PAIR, PAIR, False)
            return carry

        def masked_chunk(c, carry):
            chunk(c, 1, True)
            return carry

        whole = lax.div(full, PAIR)
        lax.fori_loop(0, whole, full_chunk, 0)
        lax.fori_loop(whole * PAIR, seen, masked_chunk, 0)
        lane = lax.broadcasted_iota(jnp.int32, (QT, HD), 1)
        lse = jnp.zeros((QT, HD), jnp.float32)
        for h in range(PER):
            total = jnp.sum(l_s[h], axis=1, keepdims=True)
            total = jnp.where(total == 0.0, 1.0, total)
            out = (acc_s[h] / total).astype(jnp.bfloat16)
            for a in range(NXT):
                for b in range(2):
                    at = pl.ds(pl.multiple_of((b * 4 + quarter_z) * TOK, TOK), TOK)
                    o_ref[part_x + a, at, h * HD : (h + 1) * HD] = out[
                        (a * 2 + b) * TOK : (a * 2 + b + 1) * TOK
                    ]
            lse = jnp.where(lane == h, m_s[h] * SCALE2 + jnp.log2(total), lse)
        for a in range(NXT):
            for b in range(2):
                at = pl.ds(pl.multiple_of((b * 4 + quarter_z) * TOK, TOK), TOK)
                lse_s[part_x + a, at, :] = lse[(a * 2 + b) * TOK : (a * 2 + b + 1) * TOK]
        return carry

    lax.fori_loop(0, 4 * NX // NXT, tile, 0)
    for a in range(NX):
        stat = jnp.concatenate(
            [lse_s[a, g * HD : (g + 1) * HD, :].T[:8] for g in range(QROWS // HD)], axis=0
        )
        for n in range(3):
            part = stat.astype(jnp.bfloat16)
            o_ref[a, QROWS:, n * HD : (n + 1) * HD] = part
            stat = stat - part.astype(jnp.float32)


def attention(ends, place, q_all, kvs):
    n_copies = 1 + 64
    hbm = pl.BlockSpec(memory_space=pl.ANY)
    smem = pl.BlockSpec(memory_space=pltpu.SMEM)
    vmem = pl.BlockSpec(memory_space=pltpu.VMEM)
    return pl.pallas_call(
        attention_kernel,
        out_shape=jax.ShapeDtypeStruct((NX, ROWS, W), jnp.bfloat16),
        in_specs=[smem, smem] + [hbm] * 11,
        out_specs=vmem,
        scratch_shapes=[
            pltpu.VMEM((NX, QROWS, W), jnp.bfloat16),
            pltpu.VMEM((8 * KT, 2 * W), jnp.bfloat16),
            pltpu.VMEM((QT, W), jnp.bfloat16),
            pltpu.VMEM((PER, QT, HD), jnp.float32),
            pltpu.VMEM((PER, QT, HD), jnp.float32),
            pltpu.VMEM((PER, QT, HD), jnp.float32),
            pltpu.VMEM((NX, QROWS, HD), jnp.float32),
            pltpu.SemaphoreType.DMA((n_copies,)),
        ],
        compiler_params=pltpu.CompilerParams(vmem_limit_bytes=58 * 1024 * 1024),
        cost_estimate=pl.CostEstimate(
            flops=1_000_000, bytes_accessed=1_000_000, transcendentals=1_000
        ),
        name="attention",
    )(ends, place, q_all, *kvs)


def combine_kernel(got_ref, o_ref):
    logs = []
    for j in range(NX):
        parts = got_ref[j, QROWS:, :].astype(jnp.float32)
        logs.append(parts[:, :HD] + parts[:, HD : 2 * HD] + parts[:, 2 * HD :])
    peak = jnp.maximum(jnp.maximum(logs[0], logs[1]), jnp.maximum(logs[2], logs[3]))
    shares = [jnp.exp2(v - peak) for v in logs]
    total = shares[0] + shares[1] + shares[2] + shares[3]
    shares = [v / total for v in shares]
    for g in range(QROWS // HD):
        rows = [v[g * 8 : (g + 1) * 8] for v in shares]
        columns = jnp.concatenate(rows + [jnp.zeros((HD - 8 * NX, HD), jnp.float32)], axis=0).T
        at = slice(g * HD, (g + 1) * HD)
        for h in range(PER):
            out = jnp.zeros((HD, HD), jnp.float32)
            for j in range(NX):
                part = got_ref[j, at, h * HD : (h + 1) * HD].astype(jnp.float32)
                out = out + part * columns[:, j * 8 + h : j * 8 + h + 1]
            o_ref[at, h * HD : (h + 1) * HD] = out.astype(jnp.bfloat16)


def combine(got):
    vmem = pl.BlockSpec(memory_space=pltpu.VMEM)
    return pl.pallas_call(
        combine_kernel,
        out_shape=jax.ShapeDtypeStruct((QROWS, W), jnp.bfloat16),
        in_specs=[vmem],
        out_specs=vmem,
        compiler_params=pltpu.CompilerParams(vmem_limit_bytes=16 * 1024 * 1024),
        cost_estimate=pl.CostEstimate(flops=4_000_000, bytes_accessed=2_500_000, transcendentals=20_000),
        name="combine",
    )(got)


def project_kernel(pos_ref, keep_ref, got_ref, *refs):
    w_in = refs[:5]
    o_ref = refs[5]
    w_s, acc_s, sems = refs[6:]
    zl = pos_ref[2]
    started = []
    wide = D // 2
    for j in range(5):
        dst = w_s.at[j] if j < 3 else w_s.at[3, :, pl.ds((j - 3) * wide, wide)]
        c = pltpu.make_async_copy(w_in[j], dst, sems.at[j])
        c.start()
        started.append(c)
    acc_s[...] = jnp.zeros_like(acc_s)
    for j, step in enumerate((0, 1, 3, 2)):
        started[j].wait()
        if j == 3:
            started[4].wait()
        row = lax.rem(zl + step, 4)
        lhs = jnp.concatenate([keep_ref[row], got_ref[row]], axis=0)
        acc_s[...] += jnp.dot(lhs, w_s[j], preferred_element_type=jnp.float32)
    o_ref[0] = acc_s[:TOK].astype(jnp.bfloat16)
    o_ref[1] = acc_s[TOK:].astype(jnp.bfloat16)


def project(place, keep, got, weights):
    vmem = pl.BlockSpec(memory_space=pltpu.VMEM)
    return pl.pallas_call(
        project_kernel,
        out_shape=jax.ShapeDtypeStruct((2, TOK, D), jnp.bfloat16),
        in_specs=[pl.BlockSpec(memory_space=pltpu.SMEM), vmem, vmem]
        + [pl.BlockSpec(memory_space=pl.ANY)] * 5,
        out_specs=vmem,
        scratch_shapes=[
            pltpu.VMEM((4, W, D), jnp.bfloat16),
            pltpu.VMEM((2 * TOK, D), jnp.float32),
            pltpu.SemaphoreType.DMA((5,)),
        ],
        compiler_params=pltpu.CompilerParams(vmem_limit_bytes=28 * 1024 * 1024),
        cost_estimate=pl.CostEstimate(
            flops=2 * TOK * D * D, bytes_accessed=10_000_000, transcendentals=0
        ),
        name="project",
    )(place, keep, got, *weights)


def after(token, arrays):
    hbm = pl.BlockSpec(memory_space=pl.ANY)

    def kernel(*refs):
        pass

    return pl.pallas_call(
        kernel,
        out_shape=[jax.ShapeDtypeStruct(a.shape, a.dtype) for a in arrays],
        in_specs=[hbm] * (1 + len(arrays)),
        out_specs=[hbm] * len(arrays),
        input_output_aliases={n + 1: n for n in range(len(arrays))},
        name="after",
    )(token, *arrays)


def ring(a, axis, step):
    return lax.ppermute(a, axis, [((i + step) % 4, i) for i in range(4)])


def swap(a):
    return lax.ppermute(a, "core", [(0, 1), (1, 0)])


SKEW = [[((y0 + z) % NY) * NZ + z for z in range(NZ)] for y0 in range(NY)]


def skewed(a):
    return lax.all_to_all(a, ("y", "zh", "zl"), 0, 0, tiled=True, axis_index_groups=SKEW)


def ring_z(a, step):
    return lax.ppermute(a, ("zh", "zl"), [((i + step) % NZ, i) for i in range(NZ)])


def local(queries, keys, values, residual, out_weight, gate_table, span_lengths, noise_levels):
    def by_group(a):
        return a.reshape(TOK, NZ, W).transpose(1, 0, 2)

    qkv = jnp.concatenate([by_group(queries), by_group(keys), by_group(values)], axis=2)
    qkv = skewed(qkv).reshape(QROWS, 3 * W)
    q, kv = qkv[:, :W], qkv[:, W:]
    kv_p, kv_m = ring(kv, "y", 1), ring(kv, "y", 3)
    half = QROWS // 2
    kv_2a = ring(kv_p[:half], "y", 1)
    kv_2b = ring(kv_m[half:], "y", 3)
    mine = [kv, kv_p, kv_m, kv_2a, kv_2b]
    other = [swap(a) for a in mine]
    q_all = lax.all_to_all(jnp.broadcast_to(q[None], (NX, QROWS, W)), "x", 0, 0, tiled=True)
    arrived = q[0, 0] == q[0, 0]
    w_late = jnp.where(arrived, out_weight, jnp.zeros_like(out_weight))
    w_p, w_m = ring_z(w_late, 1), ring_z(w_late, 7)
    ends = jnp.cumsum(span_lengths)
    y, x, zl, core = (lax.axis_index(n) for n in ("y", "x", "zl", "core"))
    z = lax.axis_index(("zh", "zl"))
    place = jnp.stack([y, x, zl, core]).astype(jnp.int32)
    sent = attention(ends, place, q_all, mine + other)
    w_p, w_m = after(sent, [w_p, w_m])
    w_2a, w_2b = ring_z(w_p[:, : D // 2], 1), ring_z(w_m[:, D // 2 :], 7)
    attn = combine(lax.all_to_all(sent, "x", 0, 0, tiled=True))
    w_2a, w_2b = after(attn, [w_2a, w_2b])
    attn = skewed(attn.reshape(NZ, TOK, W)).reshape(NZ // NC, NC, TOK, W)
    low = core == 0
    keep = jnp.where(low, attn[:, 0], attn[:, 1])
    other_attn = swap(jnp.where(low, attn[:, 1], attn[:, 0]))
    terms = project(place, keep, other_attn, [w_late, w_p, w_m, w_2a, w_2b])
    proj = terms[0].astype(jnp.float32) + swap(terms[1]).astype(jnp.float32)
    first = (((y * NX + x) * NZ + z) * NC + core) * TOK
    tok = first + jnp.arange(TOK, dtype=jnp.int32)
    tok_span = jnp.sum((tok[:, None] >= ends[None, :]).astype(jnp.int32), axis=1)
    span_ids = jnp.arange(span_lengths.shape[0], dtype=jnp.int32)
    level = jnp.sum(jnp.where(tok_span[:, None] == span_ids[None, :], noise_levels[None, :], 0), axis=1)
    level_ids = jnp.arange(gate_table.shape[0], dtype=jnp.int32)
    one_hot = (level[:, None] == level_ids[None, :]).astype(jnp.float32)
    gate = jnp.dot(one_hot, gate_table, precision=lax.Precision.HIGHEST)
    return (residual.astype(jnp.float32) + gate * proj).astype(jnp.bfloat16)


def solution(mesh):
    fine = Mesh(mesh.devices.reshape(NY, NX, 2, 4, NC), ("y", "x", "zh", "zl", "core"))
    rows = P(("y", "x", "zh", "zl", "core"), None)
    return jax.shard_map(
        local,
        mesh=fine,
        in_specs=(rows, rows, rows, rows, P(("zl", "core"), None), P(), P(), P()),
        out_specs=rows,
        check_vma=False,
    )
```
